256 devices in a mesh: dp: 4 (over x), seq: 32 (over z, y), head: 2 (over core).
Axes of the slice: x: 4, y: 4, z: 8, core: 2. Of those that a mesh axis runs over, the one named last changes fastest.
Arguments:
- queries: bfloat16 [32768, 1536], P(('dp', 'seq'), 'head'), parts along dimension 0, may hold values from -8 to 8
- keys: bfloat16 [32768, 1536], P(('dp', 'seq'), 'head'), parts along dimension 0, may hold values from -8 to 8
- values: bfloat16 [32768, 1536], P(('dp', 'seq'), 'head'), parts along dimension 0, may hold values from -18 to 18
- tile_lists: int32 [128, 8], replicated, may hold values from 0 to 127, as said below
- out_weight: bfloat16 [1536, 3072], P('head'), may hold values from -0.15625 to 0.15625
Outputs:
- mixed: bfloat16 [32768, 3072], P(('dp', 'seq', 'head')), parts along dimension 0
The draws below stay inside these ranges and needn't reach their ends.
There are 4 independent parts, one for each index of `dp`. The reference program is written for one: setup_inputs(seed, part) draws one part's arguments, and reference() takes and returns one part's arrays. A program takes and returns all parts, laid end to end along the dimension named above; an argument that names none is the same for every part. Nothing has to cross between parts.
Inputs may be any that keep to these rules, and one draw needn't show every extreme that they name: `tile_lists`: tiles come in frames of 4 consecutive tiles (a 2 x 2 grid of rows and columns). Each row lists the 8 tiles of two consecutive frames, one of which is the query tile's frame; so the query tile itself is always listed, and a listed tile's frame differs from the query tile's by at most one.
All inputs are finite; a program needn't handle non-finite values.
Results may differ from the reference program's by a relative error of at most 0.015.
Values may be sent and summed in bfloat16 or wider, within the bound.
A program may use at most 64 MiB of HBM per device.

```python
import jax
import jax.numpy as jnp
from jax import lax

D = 3072
HD = 128
HEADS = 12
TILE = 64
TILES_DEV = 4
KSEL = 8
NTILES = 128
TOKENS = 8192


def draw_queries(key, part):
    key = jax.random.fold_in(key, 1)
    return jnp.clip(jax.random.normal(key, (TOKENS, HEADS * HD), jnp.float32), -6.0, 6.0).astype(jnp.bfloat16)


def draw_keys(key, part):
    key = jax.random.fold_in(key, 2)
    return jnp.clip(jax.random.normal(key, (TOKENS, HEADS * HD), jnp.float32), -6.0, 6.0).astype(jnp.bfloat16)


def draw_tile_lists(key, part):
    key = jax.random.fold_in(key, 3)
    tiles = jnp.arange(NTILES, dtype=jnp.int32)
    frame = tiles // TILES_DEV
    back = jax.random.randint(key, (NTILES,), 0, 2, dtype=jnp.int32)
    frames = NTILES // TILES_DEV
    start = jnp.clip(frame - back, 0, frames - 2)
    columns = []
    for offset in range(2):
        for within in range(TILES_DEV):
            columns.append((start + offset) * TILES_DEV + within)
    return jnp.stack(columns, axis=1).astype(jnp.int32)


def shard_levels(own_key, dims, cuts, smallest, largest):
    level, own = 1.0, jax.random.fold_in(own_key, 6)
    for position, shards_of in cuts:
        draws = jnp.exp(jax.random.uniform(jax.random.fold_in(own, position), (shards_of,), jnp.float32, smallest / len(cuts), largest / len(cuts)))
        level = level * jnp.repeat(draws, dims[position] // shards_of).reshape([-1 if axis == position else 1 for axis in range(len(dims))])
    return level


def gaussian(key, extent, spread, limit, cuts=(), kind=jnp.bfloat16):
    factor_of = shard_levels(key, extent, cuts, -0.22, 0.18) if cuts else 1.0
    array = jax.random.normal(key, extent, jnp.float32) * spread * factor_of
    return jnp.minimum(jnp.maximum(array, -limit), limit).astype(kind)


def setup_inputs(seed: int = 0, part: int = 0) -> dict:
    splits = jax.random.split(jax.random.key(seed), 6)
    part_keys = jax.random.split(jax.random.fold_in(splits[5], part), 6)
    queries = draw_queries(jax.random.fold_in(jax.random.fold_in(splits[5], part), 71), part)
    keys = draw_keys(jax.random.fold_in(jax.random.fold_in(splits[5], part), 71), part)
    values = gaussian(part_keys[2], (TOKENS, HEADS * HD), 3.0, 18.0, ((0, 32), (1, 2)))
    tile_lists = draw_tile_lists(jax.random.fold_in(splits[5], 71), part)
    out_weight = gaussian(splits[4], (HEADS * HD, D), (HEADS * HD) ** -0.5, 0.15625, ((0, 2),))
    return {"queries": queries, "keys": keys, "values": values, "tile_lists": tile_lists, "out_weight": out_weight}


def reference(queries, keys, values, tile_lists, out_weight):
    score_scale = HD ** -0.5
    query_tiles = queries.reshape(NTILES, TILE, HEADS, HD)
    key_tiles = keys.reshape(NTILES, TILE, HEADS, HD)
    value_tiles = values.reshape(NTILES, TILE, HEADS, HD)

    def one_tile(pair):
        query_block, listed = pair
        key_block = key_tiles[listed].reshape(KSEL * TILE, HEADS, HD)
        value_block = value_tiles[listed].reshape(KSEL * TILE, HEADS, HD)
        scores = jnp.einsum('qhd,khd->qhk', query_block.astype(jnp.float32), key_block.astype(jnp.float32)) * score_scale
        maximum = jnp.max(scores, axis=-1, keepdims=True)
        weights = jnp.exp(scores - maximum)
        denominator = jnp.sum(weights, axis=-1)
        rounded = lax.optimization_barrier(weights.astype(jnp.bfloat16)).astype(jnp.float32)
        summed = jnp.einsum('qhk,khd->qhd', rounded, value_block.astype(jnp.float32))
        return (summed / denominator[..., None]).astype(jnp.bfloat16).reshape(TILE, HEADS * HD)

    attended = lax.map(one_tile, (query_tiles, tile_lists)).reshape(TOKENS, HEADS * HD)
    return jnp.dot(attended, out_weight, preferred_element_type=jnp.float32).astype(jnp.bfloat16)
```

```python
import functools

import jax
import jax.numpy as jnp
from jax import lax
from jax.experimental import pallas as pl
from jax.experimental.pallas import tpu as pltpu
from jax.sharding import PartitionSpec as P

HD = 128
TILES_DEV = 4
MESH = pl.DeviceIdType.MESH
OWN, BEFORE, AFTER = 0, 1, 2
K, V = 0, 1


def remote(src, dst, send_sem, recv_sem, device):
    return pltpu.make_async_remote_copy(
        src_ref=src,
        dst_ref=dst,
        send_sem=send_sem,
        recv_sem=recv_sem,
        device_id=device,
        device_id_type=MESH,
    )


def attend(
    heads,
    q_hbm, k_hbm, v_hbm, lists_hbm, w_hbm,
    acc, last_att, last_w,
    q, kv, w, att, pair, lists,
    load_sem, kv_send, kv_recv, w_load, w_send, w_recv, att_send, att_recv,
):
    rows = q.shape[0]
    half = rows // 2
    tile = rows // TILES_DEV
    seq, core = lax.axis_index("seq"), lax.axis_index("head")
    frames = lax.axis_size("seq")
    after, before = lax.rem(seq + 1, frames), lax.rem(seq + frames - 1, frames)
    to_after, to_before, to_sibling = {"seq": after}, {"seq": before}, {"head": 1 - core}

    loads = [
        pltpu.make_async_copy(k_hbm, kv.at[K, OWN], load_sem.at[0]),
        pltpu.make_async_copy(v_hbm, kv.at[V, OWN], load_sem.at[1]),
        pltpu.make_async_copy(q_hbm, q, load_sem.at[2]),
        pltpu.make_async_copy(lists_hbm, lists, load_sem.at[3]),
    ]
    for load in loads:
        load.start()

    barrier = pltpu.get_barrier_semaphore()
    for device in (to_after, to_before, to_sibling):
        pl.semaphore_signal(barrier, inc=1, device_id=device, device_id_type=MESH)
    pl.semaphore_wait(barrier, 3)

    def columns(h):
        return pl.ds(pl.multiple_of(h * HD, HD), HD)

    def kv_copy(h, which, way):
        device, slot = ((to_after, BEFORE), (to_before, AFTER))[way]
        index = (h * 2 + which) * 2 + way
        return remote(
            kv.at[which, OWN, :, columns(h)],
            kv.at[which, slot, :, columns(h)],
            kv_send.at[index],
            kv_recv.at[index],
            device,
        )

    def w_rows(h):
        return pl.ds(pl.multiple_of(h * HD, HD), HD)

    def w_mine(h):
        target = last_w.at[pl.ds(0, HD)] if isinstance(h, int) and h == heads - 1 else w.at[h, pl.ds(0, HD)]
        return pltpu.make_async_copy(w_hbm.at[w_rows(h)], target, w_load.at[h])

    def w_theirs(h):
        target = last_w.at[pl.ds(HD, HD)] if isinstance(h, int) and h == heads - 1 else w.at[h, pl.ds(HD, HD)]
        return remote(w_hbm.at[w_rows(h)], target, w_send.at[h], w_recv.at[h], to_sibling)

    def att_copy(h):
        target = last_att.at[:, pl.ds(HD, HD)] if isinstance(h, int) and h == heads - 1 else pair.at[h, :, pl.ds(HD, HD)]
        return remote(
            att.at[h, pl.ds(pl.multiple_of((1 - core) * half, half), half)],
            target,
            att_send.at[h],
            att_recv.at[h],
            to_sibling,
        )

    loads[0].wait()
    loads[1].wait()
    for h in range(heads):
        for which in (K, V):
            for way in (0, 1):
                kv_copy(h, which, way).start()
    for h in range(heads):
        w_mine(h).start()
        w_theirs(h).start()
    loads[2].wait()
    loads[3].wait()

    picks = []
    for t in range(TILES_DEV):
        lowest = lists[seq * TILES_DEV + t, 0]
        for j in range(1, lists.shape[1]):
            lowest = jnp.minimum(lowest, lists[seq * TILES_DEV + t, j])
        pick = jnp.where(lowest < seq * TILES_DEV, 1, 0)
        picks.append(jnp.full((tile, rows), pick, jnp.int32))
    from_before = jnp.concatenate(picks, axis=0) > 0

    def project(h):
        w_mine(h).wait()
        w_theirs(h).wait()
        att_copy(h).wait()
        term = jnp.dot(pair[h], w[h], preferred_element_type=jnp.float32)
        if isinstance(h, int) and h == 0:
            acc[...] = term
        else:
            acc[...] += term

    def head(h):
        for way in (0, 1):
            kv_copy(h, K, way).wait()
        keys = kv[K, :, :, columns(h)].reshape(3 * rows, HD)
        scores = lax.dot_general(
            q[:, columns(h)], keys, (((1,), (1,)), ((), ())), preferred_element_type=jnp.float32
        ) * (HD**-0.5)
        own = scores[:, :rows]
        other = jnp.where(from_before, scores[:, rows : 2 * rows], scores[:, 2 * rows :])
        peak = jnp.maximum(jnp.max(own, axis=1, keepdims=True), jnp.max(other, axis=1, keepdims=True))
        own, other = jnp.exp(own - peak), jnp.exp(other - peak)
        denominator = jnp.sum(own, axis=1, keepdims=True) + jnp.sum(other, axis=1, keepdims=True)
        weights = jnp.concatenate(
            [own, jnp.where(from_before, other, 0.0), jnp.where(from_before, 0.0, other)], axis=1
        ).astype(jnp.bfloat16)
        if isinstance(h, int):
            if h > 0:
                project(h - 1)
        else:
            project(h - 1)
        for way in (0, 1):
            kv_copy(h, V, way).wait()
        values = kv[V, :, :, columns(h)].reshape(3 * rows, HD)
        summed = jnp.dot(weights, values, preferred_element_type=jnp.float32)
        att[h] = (summed / denominator).astype(jnp.bfloat16)
        att_copy(h).start()
        mine = att[h, pl.ds(pl.multiple_of(core * half, half), half)]
        if isinstance(h, int) and h == heads - 1:
            last_att[:, pl.ds(0, HD)] = mine
        else:
            pair[h, :, pl.ds(0, HD)] = mine

    for h in range(heads):
        head(h)
    w_mine(heads - 1).wait()
    w_theirs(heads - 1).wait()
    att_copy(heads - 1).wait()


def finish(acc, att, w, out):
    out[...] = (acc[...] + jnp.dot(att[...], w[...], preferred_element_type=jnp.float32)).astype(out.dtype)


def on_device(queries, keys, values, tile_lists, out_weight):
    rows, columns = queries.shape
    heads, half, width = columns // HD, rows // 2, out_weight.shape[1]
    bf16 = jnp.bfloat16
    anywhere = pl.BlockSpec(memory_space=pl.ANY)
    in_vmem = pl.BlockSpec(memory_space=pltpu.VMEM)
    dma = pltpu.SemaphoreType.DMA
    acc, att, w = pl.pallas_call(
        functools.partial(attend, heads),
        out_shape=(
            pltpu.VMEM((half, width), jnp.float32),
            pltpu.VMEM((half, 2 * HD), bf16),
            pltpu.VMEM((2 * HD, width), bf16),
        ),
        in_specs=[anywhere] * 5,
        out_specs=(in_vmem, in_vmem, in_vmem),
        scratch_shapes=[
            pltpu.VMEM((rows, columns), bf16),
            pltpu.VMEM((2, 3, rows, columns), bf16),
            pltpu.VMEM((heads, 2 * HD, width), bf16),
            pltpu.VMEM((heads, rows, HD), bf16),
            pltpu.VMEM((heads, half, 2 * HD), bf16),
            pltpu.SMEM(tile_lists.shape, jnp.int32),
            dma((4,)),
            dma((heads * 4,)),
            dma((heads * 4,)),
            dma((heads,)),
            dma((heads,)),
            dma((heads,)),
            dma((heads,)),
            dma((heads,)),
        ],
        compiler_params=pltpu.CompilerParams(
            collective_id=0, has_side_effects=True, vmem_limit_bytes=48 << 20
        ),
        name="attend",
    )(queries, keys, values, tile_lists, out_weight)
    blocks = 4
    return pl.pallas_call(
        finish,
        out_shape=jax.ShapeDtypeStruct((half, width), bf16),
        grid=(blocks,),
        in_specs=[
            pl.BlockSpec((half, width // blocks), lambda i: (0, i)),
            pl.BlockSpec((half, 2 * HD), lambda i: (0, 0)),
            pl.BlockSpec((2 * HD, width // blocks), lambda i: (0, i)),
        ],
        out_specs=pl.BlockSpec((half, width // blocks), lambda i: (0, i)),
        name="finish",
    )(acc, att, w)


def solution(mesh):
    placed = (
        P(("dp", "seq"), "head"),
        P(("dp", "seq"), "head"),
        P(("dp", "seq"), "head"),
        P(),
        P("head", None),
    )
    return jax.shard_map(
        on_device,
        mesh=mesh,
        in_specs=placed,
        out_specs=P(("dp", "seq", "head"), None),
        check_vma=False,
    )
```

```python
import functools

import jax
import jax.numpy as jnp
from jax import lax
from jax.experimental import pallas as pl
from jax.experimental.pallas import tpu as pltpu
from jax.sharding import PartitionSpec as P

HD = 128
TILES_DEV = 4
MESH = pl.DeviceIdType.MESH
OWN, BEFORE, AFTER = 0, 1, 2
K, V = 0, 1


def remote(src, dst, send_sem, recv_sem, device):
    return pltpu.make_async_remote_copy(
        src_ref=src,
        dst_ref=dst,
        send_sem=send_sem,
        recv_sem=recv_sem,
        device_id=device,
        device_id_type=MESH,
    )


def attend(
    heads,
    q_hbm, k_hbm, v_hbm, lists_hbm, w_hbm,
    acc, last_att, last_w,
    q, kv, w, whole, att, pair, lists,
    load_sem, kv_send, kv_recv, w_load, w_send, w_recv, att_send, att_recv,
):
    rows = q.shape[0]
    half = rows // 2
    tile = rows // TILES_DEV
    last = heads - 1
    seq, core = lax.axis_index("seq"), lax.axis_index("head")
    frames = lax.axis_size("seq")
    has_before, has_after = seq > 0, seq < frames - 1
    to_before = {"seq": jnp.maximum(seq - 1, 0)}
    to_after = {"seq": jnp.minimum(seq + 1, frames - 1)}
    to_sibling = {"head": 1 - core}
    ways = ((to_after, BEFORE, has_after, has_before), (to_before, AFTER, has_before, has_after))

    barrier = pltpu.get_barrier_semaphore()
    for device, _, sends, _ in ways:

        @pl.when(sends)
        def _(device=device):
            pl.semaphore_signal(barrier, inc=1, device_id=device, device_id_type=MESH)

    pl.semaphore_signal(barrier, inc=1, device_id=to_sibling, device_id_type=MESH)

    def columns(h):
        return pl.ds(h * HD, HD)

    loads = []
    for source, which in ((k_hbm, K), (v_hbm, V)):
        for start, width in ((0, 1), (1, heads - 1)):
            part = pl.ds(start * HD, width * HD)
            loads.append(
                (start, which, pltpu.make_async_copy(source.at[:, part], kv.at[which, OWN, :, part], load_sem.at[len(loads)]))
            )
    loads.sort(key=lambda x: x[:2])
    q_load = pltpu.make_async_copy(q_hbm, q, load_sem.at[2 * heads])
    lists_load = pltpu.make_async_copy(lists_hbm, lists, load_sem.at[2 * heads + 1])
    for _, _, load in loads:
        load.start()
    q_load.start()
    lists_load.start()

    pl.semaphore_wait(barrier, 1 + has_before.astype(jnp.int32) + has_after.astype(jnp.int32))

    def kv_copy(h, which, way):
        device, slot, _, _ = ways[way]
        index = (h * 2 + which) * 2 + way
        source = kv.at[which, OWN, :, columns(h)]
        return remote(
            source,
            kv.at[which, slot, :, columns(h)],
            kv_send.at[index],
            kv_recv.at[index],
            device,
        )

    def kv_arrive(h, which):
        for way in (0, 1):

            @pl.when(ways[way][3])
            def _():
                kv_copy(h, which, way).wait_recv()

    def kv_sent(h, which):
        for way in (0, 1):

            @pl.when(ways[way][2])
            def _():
                kv_copy(h, which, way).wait_send()

    def w_mine(h):
        target = last_w.at[pl.ds(0, HD)] if h == last else w.at[h, pl.ds(0, HD)]
        return pltpu.make_async_copy(w_hbm.at[pl.ds(h * HD, HD)], target, w_load.at[h])

    def w_theirs(h):
        target = last_w.at[pl.ds(HD, HD)] if h == last else w.at[h, pl.ds(HD, HD)]
        return remote(w_hbm.at[pl.ds(h * HD, HD)], target, w_send.at[h], w_recv.at[h], to_sibling)

    def att_copy(h):
        target = last_att.at[:, pl.ds(HD, HD)] if h == last else pair.at[h, :, pl.ds(HD, HD)]
        return remote(att.at[h], target, att_send.at[h], att_recv.at[h], to_sibling)

    order = [(h, which) for h in range(heads) for which in (K, V)]
    for h, which in order:
        for start, kind, load in loads:
            if (start, kind) == (h, which):
                load.wait()
        for way in (0, 1):

            @pl.when(ways[way][2])
            def _():
                kv_copy(h, which, way).start()
    for h in range(heads):
        w_mine(h).start()
        w_theirs(h).start()

    for slot, there in ((BEFORE, has_before), (AFTER, has_after)):

        @pl.when(jnp.logical_not(there))
        def _():
            kv[:, slot] = jnp.zeros((2, *kv.shape[2:]), kv.dtype)

    q_load.wait()
    lists_load.wait()

    picks = []
    for t in range(TILES_DEV):
        lowest = lists[0, seq * TILES_DEV + t]
        for j in range(1, lists.shape[0]):
            lowest = jnp.minimum(lowest, lists[j, seq * TILES_DEV + t])
        pick = jnp.where(lowest < seq * TILES_DEV, 1, 0)
        picks.append(jnp.full((tile, rows), pick, jnp.int32))
    from_before = jnp.concatenate(picks, axis=0) > 0

    def project(h):
        w_mine(h).wait()
        w_theirs(h).wait()
        att_copy(h).wait()
        term = jnp.dot(pair[h], w[h], preferred_element_type=jnp.float32)
        if h == 0:
            acc[...] = term
        else:
            acc[...] += term

    theirs, mine = (pl.ds(pl.multiple_of(part * half, half), half) for part in (1 - core, core))
    for h in range(heads):
        kv_arrive(h, K)
        keys = kv[K, :, :, columns(h)].reshape(3 * rows, HD)
        scores = lax.dot_general(
            q[:, columns(h)], keys, (((1,), (1,)), ((), ())), preferred_element_type=jnp.float32
        ) * (HD**-0.5)
        own = scores[:, :rows]
        other = jnp.where(from_before, scores[:, rows : 2 * rows], scores[:, 2 * rows :])
        peak = jnp.maximum(jnp.max(own, axis=1, keepdims=True), jnp.max(other, axis=1, keepdims=True))
        own, other = jnp.exp(own - peak), jnp.exp(other - peak)
        denominator = jnp.sum(own, axis=1, keepdims=True) + jnp.sum(other, axis=1, keepdims=True)
        weights = jnp.concatenate(
            [own, jnp.where(from_before, other, 0.0), jnp.where(from_before, 0.0, other)], axis=1
        ).astype(jnp.bfloat16)
        if h > 0:
            project(h - 1)
        kv_sent(h, K)
        kv_arrive(h, V)
        values = kv[V, :, :, columns(h)].reshape(3 * rows, HD)
        summed = jnp.dot(weights, values, preferred_element_type=jnp.float32)
        whole[...] = (summed / denominator).astype(jnp.bfloat16)
        att[h] = whole[theirs]
        att_copy(h).start()
        if h == last:
            last_att[:, pl.ds(0, HD)] = whole[mine]
        else:
            pair[h, :, pl.ds(0, HD)] = whole[mine]
        kv_sent(h, V)
    w_mine(last).wait()
    w_theirs(last).wait()
    att_copy(last).wait()


def finish(blocks, acc, att, w, out, rounded, sem):
    width = out.shape[1] // blocks
    copies = []
    for b in range(blocks):
        part = pl.ds(b * width, width)
        total = acc[:, part] + jnp.dot(att[...], w[:, part], preferred_element_type=jnp.float32)
        rounded[:, part] = total.astype(out.dtype)
        copies.append(pltpu.make_async_copy(rounded.at[:, part], out.at[:, part], sem.at[b]))
        copies[-1].start()
    for copy in copies:
        copy.wait()


def on_device(queries, keys, values, tile_lists, out_weight):
    rows, columns = queries.shape
    heads, half, width = columns // HD, rows // 2, out_weight.shape[1]
    bf16 = jnp.bfloat16
    anywhere = pl.BlockSpec(memory_space=pl.ANY)
    in_vmem = pl.BlockSpec(memory_space=pltpu.VMEM)
    dma = pltpu.SemaphoreType.DMA
    kept = [
        pltpu.with_memory_space_constraint(x, pltpu.HBM)
        for x in (queries, keys, values, tile_lists.T, out_weight)
    ]
    acc, att, w = pl.pallas_call(
        functools.partial(attend, heads),
        out_shape=(
            pltpu.VMEM((half, width), jnp.float32),
            pltpu.VMEM((half, 2 * HD), bf16),
            pltpu.VMEM((2 * HD, width), bf16),
        ),
        in_specs=[pl.BlockSpec(memory_space=pltpu.HBM)] * 5,
        out_specs=(in_vmem, in_vmem, in_vmem),
        scratch_shapes=[
            pltpu.VMEM((rows, columns), bf16),
            pltpu.VMEM((2, 3, rows, columns), bf16),
            pltpu.VMEM((heads, 2 * HD, width), bf16),
            pltpu.VMEM((rows, HD), bf16),
            pltpu.VMEM((heads, half, HD), bf16),
            pltpu.VMEM((heads, half, 2 * HD), bf16),
            pltpu.SMEM(kept[3].shape, jnp.int32),
            dma((2 * heads + 2,)),
            dma((heads * 4,)),
            dma((heads * 4,)),
            dma((heads,)),
            dma((heads,)),
            dma((heads,)),
            dma((heads,)),
            dma((heads,)),
        ],
        compiler_params=pltpu.CompilerParams(
            collective_id=0, has_side_effects=True, vmem_limit_bytes=48 << 20
        ),
        name="attend",
    )(*kept)
    blocks = 4
    return pl.pallas_call(
        functools.partial(finish, blocks),
        out_shape=jax.ShapeDtypeStruct((half, width), bf16),
        in_specs=[in_vmem] * 3,
        out_specs=anywhere,
        scratch_shapes=[pltpu.VMEM((half, width), bf16), dma((blocks,))],
        name="finish",
    )(*(pltpu.with_memory_space_constraint(x, pltpu.VMEM) for x in (acc, att, w)))


def solution(mesh):
    placed = (
        P(("dp", "seq"), "head"),
        P(("dp", "seq"), "head"),
        P(("dp", "seq"), "head"),
        P(),
        P("head", None),
    )
    return jax.shard_map(
        on_device,
        mesh=mesh,
        in_specs=placed,
        out_specs=P(("dp", "seq", "head"), None),
        check_vma=False,
    )
```

```python
import functools

import jax
import jax.numpy as jnp
from jax import lax
from jax.experimental import pallas as pl
from jax.experimental.pallas import tpu as pltpu
from jax.sharding import PartitionSpec as P

HD = 128
TILES_DEV = 4
MESH = pl.DeviceIdType.MESH
OWN, BEFORE, AFTER = 0, 1, 2
K, V = 0, 1
LATE = 3


def remote(src, dst, send_sem, recv_sem, device):
    return pltpu.make_async_remote_copy(
        src_ref=src,
        dst_ref=dst,
        send_sem=send_sem,
        recv_sem=recv_sem,
        device_id=device,
        device_id_type=MESH,
    )


def attend(
    heads,
    q_hbm, k_hbm, v_hbm, lists_hbm, w_hbm,
    acc, last_att, last_w,
    q, late_q, kv, w, whole, att, pair, part_out, part_mid, part_in, own_out, own_in,
    log_out, log_mid, log_in, lists,
    load_sem, kv_send, kv_recv, q_send, q_recv, att_send, att_recv, w_load, w_send, w_recv,
    swap_send, swap_recv, own_send, own_recv, part_send, part_recv, log_send, log_recv, pass_send, pass_recv,
):
    rows = q.shape[0]
    half = rows // 2
    tile = rows // TILES_DEV
    early = heads - LATE
    last = heads - 1
    scale = HD**-0.5
    seq, core = lax.axis_index("seq"), lax.axis_index("head")
    frames = lax.axis_size("seq")
    has_before, has_after = seq > 0, seq < frames - 1
    sibling = {"head": 1 - core}
    ways = (
        ({"seq": jnp.minimum(seq + 1, frames - 1)}, BEFORE, has_after, has_before),
        ({"seq": jnp.maximum(seq - 1, 0)}, AFTER, has_before, has_after),
    )

    barrier = pltpu.get_barrier_semaphore()
    for device, _, there, _ in ways:

        @pl.when(there)
        def _(device=device):
            pl.semaphore_signal(barrier, inc=1, device_id=device, device_id_type=MESH)

    pl.semaphore_signal(barrier, inc=1, device_id=sibling, device_id_type=MESH)

    loads = [
        pltpu.make_async_copy(source, target, load_sem.at[i])
        for i, (source, target) in enumerate(
            ((q_hbm, q), (k_hbm, kv.at[K, OWN]), (v_hbm, kv.at[V, OWN]), (lists_hbm, lists))
        )
    ]
    for load in loads:
        load.start()

    pl.semaphore_wait(barrier, 1 + has_before.astype(jnp.int32) + has_after.astype(jnp.int32))

    def columns(h):
        return pl.ds(h * HD, HD)

    def kv_copy(h, which, way):
        device, slot = ways[way][:2]
        index = (h * 2 + which) * 2 + way
        return remote(
            kv.at[which, OWN, :, columns(h)],
            kv.at[which, slot, :, columns(h)],
            kv_send.at[index],
            kv_recv.at[index],
            device,
        )

    def q_copy(i, way):
        device, slot = ways[way][:2]
        index = i * 2 + way
        return remote(
            q.at[:, columns(early + i)], late_q.at[i, slot - 1], q_send.at[index], q_recv.at[index], device
        )

    def part_copy(i, way):
        device, slot = ways[way][:2]
        index = i * 2 + way
        return remote(
            part_mid.at[i, way], part_in.at[i, slot - 1], part_send.at[index], part_recv.at[index], device
        )

    def log_copy(way):
        device, slot = ways[way][:2]
        return remote(log_mid.at[1 + way], log_in.at[slot - 1], log_send.at[way], log_recv.at[way], device)

    def start(copy_of, *which):
        for way in (0, 1):

            @pl.when(ways[way][2])
            def _():
                copy_of(*which, way).start()

    def sent(copy_of, *which):
        for way in (0, 1):

            @pl.when(ways[way][2])
            def _():
                copy_of(*which, way).wait_send()

    def arrive(copy_of, *which):
        for way in (0, 1):

            @pl.when(ways[way][3])
            def _():
                copy_of(*which, way).wait_recv()

    def w_target(h, at):
        return last_w.at[pl.ds(at * HD, HD)] if h == last else w.at[h, pl.ds(at * HD, HD)]

    def w_mine(h):
        return pltpu.make_async_copy(w_hbm.at[pl.ds(h * HD, HD)], w_target(h, 0), w_load.at[h])

    def w_swap(h):
        return remote(w_hbm.at[pl.ds(h * HD, HD)], w_target(h, 1), w_send.at[h], w_recv.at[h], sibling)

    def att_swap(h):
        return remote(att.at[h], pair.at[h, :, pl.ds(HD, HD)], att_send.at[h], att_recv.at[h], sibling)

    def part_swap(i):
        return remote(
            part_out.at[i, 1 - core], part_mid.at[i, :, pl.ds(HD, HD)], swap_send.at[i], swap_recv.at[i], sibling
        )

    def own_swap(i):
        return remote(own_out.at[i, 1 - core], own_in.at[i, pl.ds(HD, HD)], own_send.at[i], own_recv.at[i], sibling)

    def log_swap():
        return remote(log_out.at[1 - core], log_mid.at[:, 1], pass_send, pass_recv, sibling)

    loads[0].wait()
    for i in range(LATE):
        start(q_copy, i)
    loads[1].wait()
    loads[2].wait()
    for h in range(early):
        start(kv_copy, h, K)
        start(kv_copy, h, V)
    for h in range(heads):
        w_mine(h).start()
        w_swap(h).start()
    loads[3].wait()

    for slot, there in ((BEFORE, has_before), (AFTER, has_after)):

        @pl.when(jnp.logical_not(there))
        def _():
            kv[:, slot] = jnp.zeros((2, *kv.shape[2:]), kv.dtype)

    picks = []
    for t in range(TILES_DEV):
        lowest = lists[0, seq * TILES_DEV + t]
        for j in range(1, lists.shape[0]):
            lowest = jnp.minimum(lowest, lists[j, seq * TILES_DEV + t])
        picks.append(jnp.where(lowest < seq * TILES_DEV, 1, 0))
    from_before = (
        jnp.concatenate([jnp.full((tile, rows), pick, jnp.int32) for pick in picks], axis=0) > 0
    )
    place = lax.broadcasted_iota(jnp.int32, (1, half), 1)
    picked = jnp.zeros((1, half), jnp.int32)
    half_tiles = TILES_DEV // 2
    for t in range(half_tiles):
        pick = jnp.where(core == 0, picks[t], picks[half_tiles + t])
        inside = jnp.logical_and(place >= t * tile, place < (t + 1) * tile)
        picked = jnp.where(inside, pick, picked)
    mine_before = picked > 0

    def serve(i):
        h = early + i
        arrive(q_copy, i)
        queries = jnp.concatenate([q[:, columns(h)], late_q[i, 0], late_q[i, 1]], axis=0)
        scores = lax.dot_general(
            kv[K, OWN, :, columns(h)], queries, (((1,), (1,)), ((), ())), preferred_element_type=jnp.float32
        ) * scale
        peak = jnp.max(scores, axis=0, keepdims=True)
        weights = jnp.exp(scores - peak)
        denominator = jnp.sum(weights, axis=0, keepdims=True)
        logs = peak + jnp.log(denominator)
        part = lax.dot_general(
            kv[V, OWN, :, columns(h)],
            weights.astype(jnp.bfloat16),
            (((0,), (0,)), ((), ())),
            preferred_element_type=jnp.float32,
        ) * (1.0 / denominator)
        for slot, frame in ((OWN, 0), (1, AFTER), (2, BEFORE)):
            for whose in (0, 1):
                first = frame * rows + whose * half
                if slot == OWN:
                    own_out[i, whose] = part[:, first : first + half]
                else:
                    part_out[i, whose, slot - 1] = part[:, first : first + half].astype(jnp.bfloat16)
                log_out[whose, slot, i] = logs[:, first : first + half]
        part_swap(i).start()
        own_swap(i).start()
        for way in (0, 1):
            part_mid[i, way, pl.ds(0, HD)] = part_out[i, core, way]

    def answer():
        log_swap().wait_recv()
        start(log_copy)
        for i in range(LATE):
            part_swap(i).wait_recv()
            start(part_copy, i)

    def project(h, both):
        w_mine(h).wait()
        w_swap(h).wait()
        term = jnp.dot(both, w[h], preferred_element_type=jnp.float32)
        if h == 0:
            acc[...] = term
        else:
            acc[...] += term

    theirs, mine = (pl.ds(pl.multiple_of(part * half, half), half) for part in (1 - core, core))

    def early_head(h):
        arrive(kv_copy, h, K)
        keys = kv[K, :, :, columns(h)].reshape(3 * rows, HD)
        scores = lax.dot_general(
            q[:, columns(h)], keys, (((1,), (1,)), ((), ())), preferred_element_type=jnp.float32
        ) * scale
        own = scores[:, :rows]
        other = jnp.where(from_before, scores[:, rows : 2 * rows], scores[:, 2 * rows :])
        peak = jnp.maximum(jnp.max(own, axis=1, keepdims=True), jnp.max(other, axis=1, keepdims=True))
        own, other = jnp.exp(own - peak), jnp.exp(other - peak)
        denominator = jnp.sum(own, axis=1, keepdims=True) + jnp.sum(other, axis=1, keepdims=True)
        weights = jnp.concatenate(
            [own, jnp.where(from_before, other, 0.0), jnp.where(from_before, 0.0, other)], axis=1
        ).astype(jnp.bfloat16)
        if h > 0:
            att_swap(h - 1).wait()
            project(h - 1, pair[h - 1])
        sent(kv_copy, h, K)
        arrive(kv_copy, h, V)
        values = kv[V, :, :, columns(h)].reshape(3 * rows, HD)
        summed = jnp.dot(weights, values, preferred_element_type=jnp.float32)
        whole[...] = (summed / denominator).astype(jnp.bfloat16)
        att[h] = whole[theirs]
        att_swap(h).start()
        pair[h, :, pl.ds(0, HD)] = whole[mine]
        sent(kv_copy, h, V)

    def shares(i):
        out = []
        for whose in (0, 1):
            other = jnp.where(mine_before, log_in[0, whose, i], log_in[1, whose, i])
            out.append(1.0 / (1.0 + jnp.exp(log_mid[OWN, whose, i] - other)))
        return out

    def merge(i, share):
        arrive(part_copy, i)
        merged = []
        for whose in (0, 1):
            some = pl.ds(whose * HD, HD)
            own = own_out[i, core] if whose == 0 else own_in[i, some]
            other = jnp.where(mine_before, part_in[i, 0, some], part_in[i, 1, some]).astype(jnp.float32)
            merged.append(own + share[whose] * (other - own))
        return jnp.concatenate(merged, axis=0).T.astype(jnp.bfloat16)

    for i in range(LATE):
        serve(i)
    log_swap().start()
    for slot in (OWN, 1, 2):
        log_mid[slot, 0] = log_out[core, slot]
    for h in range(early):
        early_head(h)
        if h == 0:
            answer()
    att_swap(early - 1).wait()
    project(early - 1, pair[early - 1])
    log_swap().wait_send()
    for i in range(LATE):
        own_swap(i).wait()
        part_swap(i).wait_send()
        sent(q_copy, i)
    sent(log_copy)
    arrive(log_copy)
    share = [shares(i) for i in range(LATE)]
    w_mine(last).wait()
    w_swap(last).wait()
    for i in range(LATE):
        both = merge(i, share[i])
        if early + i < last:
            project(early + i, both)
        else:
            last_att[...] = both
        sent(part_copy, i)


def finish(blocks, acc, att, w, out, rounded, sem):
    width = out.shape[1] // blocks
    copies = []
    for b in range(blocks):
        part = pl.ds(b * width, width)
        total = acc[:, part] + jnp.dot(att[...], w[:, part], preferred_element_type=jnp.float32)
        rounded[:, part] = total.astype(out.dtype)
        copies.append(pltpu.make_async_copy(rounded.at[:, part], out.at[:, part], sem.at[b]))
        copies[-1].start()
    for copy in copies:
        copy.wait()


def on_device(queries, keys, values, tile_lists, out_weight):
    rows, columns = queries.shape
    heads, half, width = columns // HD, rows // 2, out_weight.shape[1]
    early = heads - LATE
    bf16, f32 = jnp.bfloat16, jnp.float32
    anywhere = pl.BlockSpec(memory_space=pl.ANY)
    in_vmem = pl.BlockSpec(memory_space=pltpu.VMEM)
    dma = pltpu.SemaphoreType.DMA
    kept = [
        pltpu.with_memory_space_constraint(x, pltpu.HBM)
        for x in (queries, keys, values, tile_lists.T, out_weight)
    ]
    acc, att, w = pl.pallas_call(
        functools.partial(attend, heads),
        out_shape=(
            pltpu.VMEM((half, width), f32),
            pltpu.VMEM((half, 2 * HD), bf16),
            pltpu.VMEM((2 * HD, width), bf16),
        ),
        in_specs=[pl.BlockSpec(memory_space=pltpu.HBM)] * 5,
        out_specs=(in_vmem, in_vmem, in_vmem),
        scratch_shapes=[
            pltpu.VMEM((rows, columns), bf16),
            pltpu.VMEM((LATE, 2, rows, HD), bf16),
            pltpu.VMEM((2, 3, rows, columns), bf16),
            pltpu.VMEM((heads - 1, 2 * HD, width), bf16),
            pltpu.VMEM((rows, HD), bf16),
            pltpu.VMEM((early, half, HD), bf16),
            pltpu.VMEM((early, half, 2 * HD), bf16),
            pltpu.VMEM((LATE, 2, 2, HD, half), bf16),
            pltpu.VMEM((LATE, 2, 2 * HD, half), bf16),
            pltpu.VMEM((LATE, 2, 2 * HD, half), bf16),
            pltpu.VMEM((LATE, 2, HD, half), f32),
            pltpu.VMEM((LATE, 2 * HD, half), f32),
            pltpu.VMEM((2, 3, LATE, 1, half), f32),
            pltpu.VMEM((3, 2, LATE, 1, half), f32),
            pltpu.VMEM((2, 2, LATE, 1, half), f32),
            pltpu.SMEM(kept[3].shape, jnp.int32),
            dma((4,)),
            dma((early * 4,)),
            dma((early * 4,)),
            dma((LATE * 2,)),
            dma((LATE * 2,)),
            dma((early,)),
            dma((early,)),
            dma((heads,)),
            dma((heads,)),
            dma((heads,)),
            dma((LATE,)),
            dma((LATE,)),
            dma((LATE,)),
            dma((LATE,)),
            dma((LATE * 2,)),
            dma((LATE * 2,)),
            dma((2,)),
            dma((2,)),
            dma,
            dma,
        ],
        compiler_params=pltpu.CompilerParams(
            collective_id=0, has_side_effects=True, vmem_limit_bytes=48 << 20
        ),
        name="attend",
    )(*kept)
    blocks = 4
    return pl.pallas_call(
        functools.partial(finish, blocks),
        out_shape=jax.ShapeDtypeStruct((half, width), bf16),
        in_specs=[in_vmem] * 3,
        out_specs=anywhere,
        scratch_shapes=[pltpu.VMEM((half, width), bf16), dma((blocks,))],
        name="finish",
    )(*(pltpu.with_memory_space_constraint(x, pltpu.VMEM) for x in (acc, att, w)))


def solution(mesh):
    placed = (
        P(("dp", "seq"), "head"),
        P(("dp", "seq"), "head"),
        P(("dp", "seq"), "head"),
        P(),
        P("head", None),
    )
    return jax.shard_map(
        on_device,
        mesh=mesh,
        in_specs=placed,
        out_specs=P(("dp", "seq", "head"), None),
        check_vma=False,
    )
```

```python
import functools

import jax
import jax.numpy as jnp
from jax import lax
from jax.experimental import pallas as pl
from jax.experimental.pallas import tpu as pltpu
from jax.sharding import PartitionSpec as P

HD = 128
TILES_DEV = 4
MESH = pl.DeviceIdType.MESH
OWN, BEFORE, AFTER = 0, 1, 2
K, V = 0, 1
LATE = 3
RING = 4
AT_ONCE = 3
RELAYED = 128


def remote(src, dst, send_sem, recv_sem, device):
    return pltpu.make_async_remote_copy(
        src_ref=src,
        dst_ref=dst,
        send_sem=send_sem,
        recv_sem=recv_sem,
        device_id=device,
        device_id_type=MESH,
    )


def attend(
    heads,
    q_hbm, k_hbm, v_hbm, lists_hbm, w_hbm,
    acc, last_att, last_w,
    q, late_q, kv, w, whole, att, pair, part_out, part_mid, part_in, own_out, own_in,
    log_out, log_mid, log_in, relay, lists,
    load_sem, kv_send, kv_recv, q_send, q_recv, att_send, att_recv, w_load, w_send, w_recv,
    swap_send, swap_recv, own_send, own_recv, part_send, part_recv, log_send, log_recv, pass_send, pass_recv,
    piece_send, piece_recv, relay_send, relay_recv,
):
    rows = q.shape[0]
    half = rows // 2
    tile = rows // TILES_DEV
    early = heads - LATE
    last = heads - 1
    scale = HD**-0.5
    seq, core = lax.axis_index("seq"), lax.axis_index("head")
    frames = lax.axis_size("seq")
    has_before, has_after = seq > 0, seq < frames - 1
    sibling = {"head": 1 - core}
    ways = (
        ({"seq": jnp.minimum(seq + 1, frames - 1)}, BEFORE, has_after, has_before),
        ({"seq": jnp.maximum(seq - 1, 0)}, AFTER, has_before, has_after),
    )

    place = lax.rem(seq, RING)
    next_ring, last_ring = seq < frames - RING, seq >= RING
    joins = ((0, jnp.logical_and(place == 3, next_ring)), (1, jnp.logical_and(place == 0, last_ring)))
    near = ((0, jnp.logical_and(place == 2, next_ring)), (1, jnp.logical_and(place == 1, last_ring)))
    far = ((0, jnp.logical_and(place == 1, next_ring)), (1, jnp.logical_and(place == 2, last_ring)))
    over = (
        {"seq": jnp.minimum(seq + RING - 1, frames - 1)},
        {"seq": jnp.maximum(seq - RING + 1, 0)},
    )

    barrier = pltpu.get_barrier_semaphore()
    for device, _, there, _ in ways:

        @pl.when(there)
        def _(device=device):
            pl.semaphore_signal(barrier, inc=1, device_id=device, device_id_type=MESH)

    pl.semaphore_signal(barrier, inc=1, device_id=sibling, device_id_type=MESH)

    loads = [
        pltpu.make_async_copy(source, target, load_sem.at[i])
        for i, (source, target) in enumerate(
            ((q_hbm, q), (k_hbm, kv.at[K, OWN]), (v_hbm, kv.at[V, OWN]), (lists_hbm, lists))
        )
    ]
    for load in loads:
        load.start()

    pl.semaphore_wait(barrier, 1 + has_before.astype(jnp.int32) + has_after.astype(jnp.int32))

    def columns(h):
        return pl.ds(h * HD, HD)

    size = relay.shape[1]
    piece_at = (V, pl.ds(0, size), columns(early - 1))

    def kv_copy(h, which, way):
        device, slot = ways[way][:2]
        index = (h * 2 + which) * 2 + way
        some = pl.ds(size, rows - size) if (h, which) == (early - 1, V) else pl.ds(0, rows)
        return remote(
            kv.at[which, OWN, some, columns(h)],
            kv.at[which, slot, some, columns(h)],
            kv_send.at[index],
            kv_recv.at[index],
            device,
        )

    def piece(slot):
        return kv.at[piece_at[0], slot, piece_at[1], piece_at[2]]

    def piece_copy(way):
        device, slot = ways[way][:2]
        return remote(piece(OWN), piece(slot), piece_send.at[way], piece_recv.at[way], device)

    def to_relay(way):
        return remote(piece(OWN), relay.at[way], piece_send.at[way], relay_recv.at[way], ways[1 - way][0])

    def relay_on(way):
        return remote(relay.at[way], relay.at[way], relay_send.at[way], relay_recv.at[way], ways[1 - way][0])

    def relay_out(way):
        slot = ways[way][1]
        return remote(relay.at[way], piece(slot), relay_send.at[way], piece_recv.at[way], over[way])

    def q_copy(i, way):
        device, slot = ways[way][:2]
        index = i * 2 + way
        return remote(
            q.at[:, columns(early + i)], late_q.at[i, slot - 1], q_send.at[index], q_recv.at[index], device
        )

    def part_copy(i, way):
        device, slot = ways[way][:2]
        index = i * 2 + way
        return remote(
            part_mid.at[i, way], part_in.at[i, slot - 1], part_send.at[index], part_recv.at[index], device
        )

    def log_copy(way):
        device, slot = ways[way][:2]
        return remote(log_mid.at[1 + way], log_in.at[slot - 1], log_send.at[way], log_recv.at[way], device)

    def start(copy_of, *which):
        for way in (0, 1):

            @pl.when(ways[way][2])
            def _():
                copy_of(*which, way).start()

    def sent(copy_of, *which):
        for way in (0, 1):

            @pl.when(ways[way][2])
            def _():
                copy_of(*which, way).wait_send()

    def arrive(copy_of, *which):
        for way in (0, 1):

            @pl.when(ways[way][3])
            def _():
                copy_of(*which, way).wait_recv()

    def w_target(h, at):
        return last_w.at[pl.ds(at * HD, HD)] if h == last else w.at[h, pl.ds(at * HD, HD)]

    def w_mine(h):
        return pltpu.make_async_copy(w_hbm.at[pl.ds(h * HD, HD)], w_target(h, 0), w_load.at[h])

    def w_swap(h):
        return remote(w_hbm.at[pl.ds(h * HD, HD)], w_target(h, 1), w_send.at[h], w_recv.at[h], sibling)

    def att_swap(h):
        return remote(att.at[h], pair.at[h, :, pl.ds(HD, HD)], att_send.at[h], att_recv.at[h], sibling)

    def part_swap(i):
        return remote(
            part_out.at[i, 1 - core], part_mid.at[i, :, pl.ds(HD, HD)], swap_send.at[i], swap_recv.at[i], sibling
        )

    def own_swap(i):
        return remote(own_out.at[i, 1 - core], own_in.at[i, pl.ds(HD, HD)], own_send.at[i], own_recv.at[i], sibling)

    def log_swap():
        return remote(log_out.at[1 - core], log_mid.at[:, 1], pass_send, pass_recv, sibling)

    for load in loads[:3]:
        load.wait()
    for way, there in joins:

        @pl.when(there)
        def _():
            to_relay(way).start()

    for i in range(LATE):
        start(q_copy, i)
    queue = [(h, which) for h in range(early) for which in (K, V)]
    for h, which in queue[:AT_ONCE]:
        start(kv_copy, h, which)
    for h in range(heads):
        w_mine(h).start()
        w_swap(h).start()
    loads[3].wait()

    for slot, there in ((BEFORE, has_before), (AFTER, has_after)):

        @pl.when(jnp.logical_not(there))
        def _():
            kv[:, slot] = jnp.zeros((2, *kv.shape[2:]), kv.dtype)

    picks = []
    for t in range(TILES_DEV):
        lowest = lists[0, seq * TILES_DEV + t]
        for j in range(1, lists.shape[0]):
            lowest = jnp.minimum(lowest, lists[j, seq * TILES_DEV + t])
        picks.append(jnp.where(lowest < seq * TILES_DEV, 1, 0))
    from_before = (
        jnp.concatenate([jnp.full((tile, rows), pick, jnp.int32) for pick in picks], axis=0) > 0
    )
    token = lax.broadcasted_iota(jnp.int32, (1, half), 1)
    picked = jnp.zeros((1, half), jnp.int32)
    half_tiles = TILES_DEV // 2
    for t in range(half_tiles):
        pick = jnp.where(core == 0, picks[t], picks[half_tiles + t])
        inside = jnp.logical_and(token >= t * tile, token < (t + 1) * tile)
        picked = jnp.where(inside, pick, picked)
    mine_before = picked > 0

    def serve(i):
        h = early + i
        arrive(q_copy, i)
        queries = jnp.concatenate([q[:, columns(h)], late_q[i, 0], late_q[i, 1]], axis=0)
        scores = lax.dot_general(
            kv[K, OWN, :, columns(h)], queries, (((1,), (1,)), ((), ())), preferred_element_type=jnp.float32
        ) * scale
        peak = jnp.max(scores, axis=0, keepdims=True)
        weights = jnp.exp(scores - peak)
        denominator = jnp.sum(weights, axis=0, keepdims=True)
        logs = peak + jnp.log(denominator)
        part = lax.dot_general(
            kv[V, OWN, :, columns(h)],
            weights.astype(jnp.bfloat16),
            (((0,), (0,)), ((), ())),
            preferred_element_type=jnp.float32,
        ) * (1.0 / denominator)
        for slot, frame in ((OWN, 0), (1, AFTER), (2, BEFORE)):
            for whose in (0, 1):
                first = frame * rows + whose * half
                if slot == OWN:
                    own_out[i, whose] = part[:, first : first + half]
                else:
                    part_out[i, whose, slot - 1] = part[:, first : first + half].astype(jnp.bfloat16)
                log_out[whose, slot, i] = logs[:, first : first + half]
        part_swap(i).start()
        own_swap(i).start()
        for way in (0, 1):
            part_mid[i, way, pl.ds(0, HD)] = part_out[i, core, way]

    def answer():
        log_swap().wait_recv()
        start(log_copy)
        for i in range(LATE):
            part_swap(i).wait_recv()
            start(part_copy, i)

    def project(h, both):
        w_mine(h).wait()
        w_swap(h).wait()
        term = jnp.dot(both, w[h], preferred_element_type=jnp.float32)
        if h == 0:
            acc[...] = term
        else:
            acc[...] += term

    theirs, mine = (pl.ds(pl.multiple_of(part * half, half), half) for part in (1 - core, core))

    def early_head(h):
        arrive(kv_copy, h, K)
        keys = kv[K, :, :, columns(h)].reshape(3 * rows, HD)
        scores = lax.dot_general(
            q[:, columns(h)], keys, (((1,), (1,)), ((), ())), preferred_element_type=jnp.float32
        ) * scale
        own = scores[:, :rows]
        other = jnp.where(from_before, scores[:, rows : 2 * rows], scores[:, 2 * rows :])
        peak = jnp.maximum(jnp.max(own, axis=1, keepdims=True), jnp.max(other, axis=1, keepdims=True))
        own, other = jnp.exp(own - peak), jnp.exp(other - peak)
        denominator = jnp.sum(own, axis=1, keepdims=True) + jnp.sum(other, axis=1, keepdims=True)
        weights = jnp.concatenate(
            [own, jnp.where(from_before, other, 0.0), jnp.where(from_before, 0.0, other)], axis=1
        ).astype(jnp.bfloat16)
        if h > 0:
            att_swap(h - 1).wait()
            project(h - 1, pair[h - 1])
        sent(kv_copy, h, K)
        arrive(kv_copy, h, V)
        if h == early - 1:
            arrive(piece_copy)
        values = kv[V, :, :, columns(h)].reshape(3 * rows, HD)
        summed = jnp.dot(weights, values, preferred_element_type=jnp.float32)
        whole[...] = (summed / denominator).astype(jnp.bfloat16)
        att[h] = whole[theirs]
        att_swap(h).start()
        pair[h, :, pl.ds(0, HD)] = whole[mine]
        sent(kv_copy, h, V)

    def shares(i):
        out = []
        for whose in (0, 1):
            other = jnp.where(mine_before, log_in[0, whose, i], log_in[1, whose, i])
            out.append(1.0 / (1.0 + jnp.exp(log_mid[OWN, whose, i] - other)))
        return out

    def merge(i, share):
        arrive(part_copy, i)
        merged = []
        for whose in (0, 1):
            some = pl.ds(whose * HD, HD)
            own = own_out[i, core] if whose == 0 else own_in[i, some]
            other = jnp.where(mine_before, part_in[i, 0, some], part_in[i, 1, some]).astype(jnp.float32)
            merged.append(own + share[whose] * (other - own))
        return jnp.concatenate(merged, axis=0).T.astype(jnp.bfloat16)

    def pass_on(copy_of, relays):
        for way, there in relays:

            @pl.when(there)
            def _():
                relay_on(way).wait_recv()
                copy_of(way).start()

    for i in range(LATE):
        serve(i)
        if i == 0:
            pass_on(relay_on, near)
            for h, which in queue[AT_ONCE:]:
                if (h, which) == (early - 1, V):
                    for way, there in joins:

                        @pl.when(jnp.logical_and(ways[way][2], jnp.logical_not(there)))
                        def _():
                            piece_copy(way).start()

                start(kv_copy, h, which)
    log_swap().start()
    for slot in (OWN, 1, 2):
        log_mid[slot, 0] = log_out[core, slot]
    for h in range(early):
        early_head(h)
        if h == 0:
            for way, there in near:

                @pl.when(there)
                def _():
                    relay_on(way).wait_send()

            pass_on(relay_out, far)
            answer()
    att_swap(early - 1).wait()
    project(early - 1, pair[early - 1])
    log_swap().wait_send()
    sent(piece_copy)
    for way, there in far:

        @pl.when(there)
        def _():
            relay_out(way).wait_send()

    for i in range(LATE):
        own_swap(i).wait()
        part_swap(i).wait_send()
        sent(q_copy, i)
    sent(log_copy)
    arrive(log_copy)
    share = [shares(i) for i in range(LATE)]
    w_mine(last).wait()
    w_swap(last).wait()
    for i in range(LATE):
        both = merge(i, share[i])
        if early + i < last:
            project(early + i, both)
        else:
            last_att[...] = both
        sent(part_copy, i)


def finish(blocks, acc, att, w, out, rounded, sem):
    width = out.shape[1] // blocks
    copies = []
    for b in range(blocks):
        part = pl.ds(b * width, width)
        total = acc[:, part] + jnp.dot(att[...], w[:, part], preferred_element_type=jnp.float32)
        rounded[:, part] = total.astype(out.dtype)
        copies.append(pltpu.make_async_copy(rounded.at[:, part], out.at[:, part], sem.at[b]))
        copies[-1].start()
    for copy in copies:
        copy.wait()


def on_device(queries, keys, values, tile_lists, out_weight):
    rows, columns = queries.shape
    heads, half, width = columns // HD, rows // 2, out_weight.shape[1]
    early = heads - LATE
    bf16, f32 = jnp.bfloat16, jnp.float32
    anywhere = pl.BlockSpec(memory_space=pl.ANY)
    in_vmem = pl.BlockSpec(memory_space=pltpu.VMEM)
    dma = pltpu.SemaphoreType.DMA
    kept = [
        pltpu.with_memory_space_constraint(x, pltpu.HBM)
        for x in (queries, keys, values, tile_lists.T, out_weight)
    ]
    acc, att, w = pl.pallas_call(
        functools.partial(attend, heads),
        out_shape=(
            pltpu.VMEM((half, width), f32),
            pltpu.VMEM((half, 2 * HD), bf16),
            pltpu.VMEM((2 * HD, width), bf16),
        ),
        in_specs=[pl.BlockSpec(memory_space=pltpu.HBM)] * 5,
        out_specs=(in_vmem, in_vmem, in_vmem),
        scratch_shapes=[
            pltpu.VMEM((rows, columns), bf16),
            pltpu.VMEM((LATE, 2, rows, HD), bf16),
            pltpu.VMEM((2, 3, rows, columns), bf16),
            pltpu.VMEM((heads - 1, 2 * HD, width), bf16),
            pltpu.VMEM((rows, HD), bf16),
            pltpu.VMEM((early, half, HD), bf16),
            pltpu.VMEM((early, half, 2 * HD), bf16),
            pltpu.VMEM((LATE, 2, 2, HD, half), bf16),
            pltpu.VMEM((LATE, 2, 2 * HD, half), bf16),
            pltpu.VMEM((LATE, 2, 2 * HD, half), bf16),
            pltpu.VMEM((LATE, 2, HD, half), f32),
            pltpu.VMEM((LATE, 2 * HD, half), f32),
            pltpu.VMEM((2, 3, LATE, 1, half), f32),
            pltpu.VMEM((3, 2, LATE, 1, half), f32),
            pltpu.VMEM((2, 2, LATE, 1, half), f32),
            pltpu.VMEM((2, RELAYED, HD), bf16),
            pltpu.SMEM(kept[3].shape, jnp.int32),
            dma((4,)),
            dma((early * 4,)),
            dma((early * 4,)),
            dma((LATE * 2,)),
            dma((LATE * 2,)),
            dma((early,)),
            dma((early,)),
            dma((heads,)),
            dma((heads,)),
            dma((heads,)),
            dma((LATE,)),
            dma((LATE,)),
            dma((LATE,)),
            dma((LATE,)),
            dma((LATE * 2,)),
            dma((LATE * 2,)),
            dma((2,)),
            dma((2,)),
            dma,
            dma,
            dma((2,)),
            dma((2,)),
            dma((2,)),
            dma((2,)),
        ],
        compiler_params=pltpu.CompilerParams(
            collective_id=0, has_side_effects=True, vmem_limit_bytes=48 << 20
        ),
        name="attend",
    )(*kept)
    blocks = 4
    return pl.pallas_call(
        functools.partial(finish, blocks),
        out_shape=jax.ShapeDtypeStruct((half, width), bf16),
        in_specs=[in_vmem] * 3,
        out_specs=anywhere,
        scratch_shapes=[pltpu.VMEM((half, width), bf16), dma((blocks,))],
        name="finish",
    )(*(pltpu.with_memory_space_constraint(x, pltpu.VMEM) for x in (acc, att, w)))


def solution(mesh):
    placed = (
        P(("dp", "seq"), "head"),
        P(("dp", "seq"), "head"),
        P(("dp", "seq"), "head"),
        P(),
        P("head", None),
    )
    return jax.shard_map(
        on_device,
        mesh=mesh,
        in_specs=placed,
        out_specs=P(("dp", "seq", "head"), None),
        check_vma=False,
    )
```

```python
import functools

import jax
import jax.numpy as jnp
from jax import lax
from jax.experimental import pallas as pl
from jax.experimental.pallas import tpu as pltpu
from jax.sharding import PartitionSpec as P

HD = 128
TILES_DEV = 4
MESH = pl.DeviceIdType.MESH
OWN, BEFORE, AFTER = 0, 1, 2
K, V = 0, 1
LATE = 3
RING = 4
AT_ONCE = 2
RELAYED = 128


def remote(src, dst, send_sem, recv_sem, device):
    return pltpu.make_async_remote_copy(
        src_ref=src,
        dst_ref=dst,
        send_sem=send_sem,
        recv_sem=recv_sem,
        device_id=device,
        device_id_type=MESH,
    )


def attend(
    heads,
    q_hbm, k_hbm, v_hbm, lists_hbm, w_hbm,
    acc, last_att, last_w,
    q, late_q, kv, w, whole, att, pair, part_out, part_mid, part_in, own_out, own_in,
    log_out, log_mid, log_in, relay, lists,
    load_sem, kv_send, kv_recv, q_send, q_recv, att_send, att_recv, w_load, w_send, w_recv,
    swap_send, swap_recv, own_send, own_recv, part_send, part_recv, log_send, log_recv, pass_send, pass_recv,
    piece_send, piece_recv, relay_send, relay_recv,
):
    rows = q.shape[0]
    half = rows // 2
    tile = rows // TILES_DEV
    early = heads - LATE
    last = heads - 1
    scale = HD**-0.5
    seq, core = lax.axis_index("seq"), lax.axis_index("head")
    frames = lax.axis_size("seq")
    has_before, has_after = seq > 0, seq < frames - 1
    sibling = {"head": 1 - core}
    ways = (
        ({"seq": jnp.minimum(seq + 1, frames - 1)}, BEFORE, has_after, has_before),
        ({"seq": jnp.maximum(seq - 1, 0)}, AFTER, has_before, has_after),
    )

    place = lax.rem(seq, RING)
    next_ring, last_ring = seq < frames - RING, seq >= RING
    joins = ((0, jnp.logical_and(place == 3, next_ring)), (1, jnp.logical_and(place == 0, last_ring)))
    near = ((0, jnp.logical_and(place == 2, next_ring)), (1, jnp.logical_and(place == 1, last_ring)))
    far = ((0, jnp.logical_and(place == 1, next_ring)), (1, jnp.logical_and(place == 2, last_ring)))
    over = (
        {"seq": jnp.minimum(seq + RING - 1, frames - 1)},
        {"seq": jnp.maximum(seq - RING + 1, 0)},
    )

    barrier = pltpu.get_barrier_semaphore()
    for device, _, there, _ in ways:

        @pl.when(there)
        def _(device=device):
            pl.semaphore_signal(barrier, inc=1, device_id=device, device_id_type=MESH)

    pl.semaphore_signal(barrier, inc=1, device_id=sibling, device_id_type=MESH)

    loads = [
        pltpu.make_async_copy(source, target, load_sem.at[i])
        for i, (source, target) in enumerate(
            ((q_hbm, q), (k_hbm, kv.at[K, OWN]), (v_hbm, kv.at[V, OWN]), (lists_hbm, lists))
        )
    ]
    for load in loads:
        load.start()

    pl.semaphore_wait(barrier, 1 + has_before.astype(jnp.int32) + has_after.astype(jnp.int32))

    def columns(h):
        return pl.ds(h * HD, HD)

    size = relay.shape[1]
    piece_at = (V, pl.ds(0, size), columns(early - 1))

    def kv_copy(h, which, way):
        device, slot = ways[way][:2]
        index = (h * 2 + which) * 2 + way
        some = pl.ds(size, rows - size) if (h, which) == (early - 1, V) else pl.ds(0, rows)
        return remote(
            kv.at[which, OWN, some, columns(h)],
            kv.at[which, slot, some, columns(h)],
            kv_send.at[index],
            kv_recv.at[index],
            device,
        )

    def piece(slot):
        return kv.at[piece_at[0], slot, piece_at[1], piece_at[2]]

    def piece_copy(way):
        device, slot = ways[way][:2]
        return remote(piece(OWN), piece(slot), piece_send.at[way], piece_recv.at[way], device)

    def to_relay(way):
        return remote(piece(OWN), relay.at[way], piece_send.at[way], relay_recv.at[way], ways[1 - way][0])

    def relay_on(way):
        return remote(relay.at[way], relay.at[way], relay_send.at[way], relay_recv.at[way], ways[1 - way][0])

    def relay_out(way):
        slot = ways[way][1]
        return remote(relay.at[way], piece(slot), relay_send.at[way], piece_recv.at[way], over[way])

    def q_copy(i, way):
        device, slot = ways[way][:2]
        index = i * 2 + way
        return remote(
            q.at[:, columns(early + i)], late_q.at[i, slot - 1], q_send.at[index], q_recv.at[index], device
        )

    def part_copy(i, way):
        device, slot = ways[way][:2]
        index = i * 2 + way
        return remote(
            part_mid.at[i, way], part_in.at[i, slot - 1], part_send.at[index], part_recv.at[index], device
        )

    def log_copy(way):
        device, slot = ways[way][:2]
        return remote(log_mid.at[1 + way], log_in.at[slot - 1], log_send.at[way], log_recv.at[way], device)

    def start(copy_of, *which):
        for way in (0, 1):

            @pl.when(ways[way][2])
            def _():
                copy_of(*which, way).start()

    def sent(copy_of, *which):
        for way in (0, 1):

            @pl.when(ways[way][2])
            def _():
                copy_of(*which, way).wait_send()

    def arrive(copy_of, *which):
        for way in (0, 1):

            @pl.when(ways[way][3])
            def _():
                copy_of(*which, way).wait_recv()

    def w_target(h, at):
        return last_w.at[pl.ds(at * HD, HD)] if h == last else w.at[h, pl.ds(at * HD, HD)]

    def w_mine(h):
        return pltpu.make_async_copy(w_hbm.at[pl.ds(h * HD, HD)], w_target(h, 0), w_load.at[h])

    def w_swap(h):
        return remote(w_hbm.at[pl.ds(h * HD, HD)], w_target(h, 1), w_send.at[h], w_recv.at[h], sibling)

    def att_swap(h):
        return remote(att.at[h], pair.at[h, :, pl.ds(HD, HD)], att_send.at[h], att_recv.at[h], sibling)

    def part_swap(i):
        return remote(
            part_out.at[i, 1 - core], part_mid.at[i, :, pl.ds(HD, HD)], swap_send.at[i], swap_recv.at[i], sibling
        )

    def own_swap(i):
        return remote(own_out.at[i, 1 - core], own_in.at[i, pl.ds(HD, HD)], own_send.at[i], own_recv.at[i], sibling)

    def log_swap():
        return remote(log_out.at[1 - core], log_mid.at[:, 1], pass_send, pass_recv, sibling)

    for load in loads[:3]:
        load.wait()
    for way, there in joins:

        @pl.when(there)
        def _():
            to_relay(way).start()

    for i in range(LATE):
        start(q_copy, i)
    queue = [(h, which) for h in range(early) for which in (K, V)]
    for h, which in queue[:AT_ONCE]:
        start(kv_copy, h, which)
    for h in range(heads):
        w_mine(h).start()
        if h < early:
            w_swap(h).start()
    loads[3].wait()

    for slot, there in ((BEFORE, has_before), (AFTER, has_after)):

        @pl.when(jnp.logical_not(there))
        def _():
            kv[:, slot] = jnp.zeros((2, *kv.shape[2:]), kv.dtype)

    picks = []
    for t in range(TILES_DEV):
        lowest = lists[0, seq * TILES_DEV + t]
        for j in range(1, lists.shape[0]):
            lowest = jnp.minimum(lowest, lists[j, seq * TILES_DEV + t])
        picks.append(jnp.where(lowest < seq * TILES_DEV, 1, 0))
    from_before = (
        jnp.concatenate([jnp.full((tile, rows), pick, jnp.int32) for pick in picks], axis=0) > 0
    )
    token = lax.broadcasted_iota(jnp.int32, (1, half), 1)
    picked = jnp.zeros((1, half), jnp.int32)
    half_tiles = TILES_DEV // 2
    for t in range(half_tiles):
        pick = jnp.where(core == 0, picks[t], picks[half_tiles + t])
        inside = jnp.logical_and(token >= t * tile, token < (t + 1) * tile)
        picked = jnp.where(inside, pick, picked)
    mine_before = picked > 0

    def serve(i):
        h = early + i
        arrive(q_copy, i)
        queries = jnp.concatenate([q[:, columns(h)], late_q[i, 0], late_q[i, 1]], axis=0)
        scores = lax.dot_general(
            kv[K, OWN, :, columns(h)], queries, (((1,), (1,)), ((), ())), preferred_element_type=jnp.float32
        ) * scale
        peak = jnp.max(scores, axis=0, keepdims=True)
        weights = jnp.exp(scores - peak)
        denominator = jnp.sum(weights, axis=0, keepdims=True)
        logs = peak + jnp.log(denominator)
        part = lax.dot_general(
            kv[V, OWN, :, columns(h)],
            weights.astype(jnp.bfloat16),
            (((0,), (0,)), ((), ())),
            preferred_element_type=jnp.float32,
        ) * (1.0 / denominator)
        for slot, frame in ((OWN, 0), (1, AFTER), (2, BEFORE)):
            for whose in (0, 1):
                first = frame * rows + whose * half
                if slot == OWN:
                    own_out[i, whose] = part[:, first : first + half]
                else:
                    part_out[i, whose, slot - 1] = part[:, first : first + half].astype(jnp.bfloat16)
                log_out[whose, slot, i] = logs[:, first : first + half]
        part_swap(i).start()
        own_swap(i).start()
        for way in (0, 1):
            part_mid[i, way, pl.ds(0, HD)] = part_out[i, core, way]

    def answer():
        log_swap().wait_recv()
        start(log_copy)
        for i in range(LATE):
            part_swap(i).wait_recv()
            start(part_copy, i)

    def project(h, both):
        w_mine(h).wait()
        w_swap(h).wait()
        term = jnp.dot(both, w[h], preferred_element_type=jnp.float32)
        if h == 0:
            acc[...] = term
        else:
            acc[...] += term

    theirs, mine = (pl.ds(pl.multiple_of(part * half, half), half) for part in (1 - core, core))

    def early_head(h):
        arrive(kv_copy, h, K)
        keys = kv[K, :, :, columns(h)].reshape(3 * rows, HD)
        scores = lax.dot_general(
            q[:, columns(h)], keys, (((1,), (1,)), ((), ())), preferred_element_type=jnp.float32
        ) * scale
        own = scores[:, :rows]
        other = jnp.where(from_before, scores[:, rows : 2 * rows], scores[:, 2 * rows :])
        peak = jnp.maximum(jnp.max(own, axis=1, keepdims=True), jnp.max(other, axis=1, keepdims=True))
        own, other = jnp.exp(own - peak), jnp.exp(other - peak)
        denominator = jnp.sum(own, axis=1, keepdims=True) + jnp.sum(other, axis=1, keepdims=True)
        weights = jnp.concatenate(
            [own, jnp.where(from_before, other, 0.0), jnp.where(from_before, 0.0, other)], axis=1
        ).astype(jnp.bfloat16)
        if h > 0:
            att_swap(h - 1).wait()
            project(h - 1, pair[h - 1])
        sent(kv_copy, h, K)
        arrive(kv_copy, h, V)
        if h == early - 1:
            arrive(piece_copy)
        values = kv[V, :, :, columns(h)].reshape(3 * rows, HD)
        summed = jnp.dot(weights, values, preferred_element_type=jnp.float32)
        whole[...] = (summed / denominator).astype(jnp.bfloat16)
        att[h] = whole[theirs]
        att_swap(h).start()
        pair[h, :, pl.ds(0, HD)] = whole[mine]
        sent(kv_copy, h, V)

    def shares(i):
        out = []
        for whose in (0, 1):
            other = jnp.where(mine_before, log_in[0, whose, i], log_in[1, whose, i])
            out.append(1.0 / (1.0 + jnp.exp(log_mid[OWN, whose, i] - other)))
        return out

    def merge(i, share):
        arrive(part_copy, i)
        merged = []
        for whose in (0, 1):
            some = pl.ds(whose * HD, HD)
            own = own_out[i, core] if whose == 0 else own_in[i, some]
            other = jnp.where(mine_before, part_in[i, 0, some], part_in[i, 1, some]).astype(jnp.float32)
            merged.append(own + share[whose] * (other - own))
        return jnp.concatenate(merged, axis=0).T.astype(jnp.bfloat16)

    def pass_on(copy_of, relays):
        for way, there in relays:

            @pl.when(there)
            def _():
                relay_on(way).wait_recv()
                copy_of(way).start()

    for i in range(LATE):
        serve(i)
        if i == 0:
            pass_on(relay_on, near)
            for h, which in queue[AT_ONCE:]:
                if (h, which) == (early - 1, V):
                    for way, there in joins:

                        @pl.when(jnp.logical_and(ways[way][2], jnp.logical_not(there)))
                        def _():
                            piece_copy(way).start()

                start(kv_copy, h, which)
    log_swap().start()
    for slot in (OWN, 1, 2):
        log_mid[slot, 0] = log_out[core, slot]
    answer()
    for h in range(early, heads):
        w_swap(h).start()
    for h in range(early):
        early_head(h)
        if h == 0:
            for way, there in near:

                @pl.when(there)
                def _():
                    relay_on(way).wait_send()

            pass_on(relay_out, far)
    att_swap(early - 1).wait()
    project(early - 1, pair[early - 1])
    log_swap().wait_send()
    sent(piece_copy)
    for way, there in far:

        @pl.when(there)
        def _():
            relay_out(way).wait_send()

    for i in range(LATE):
        own_swap(i).wait()
        part_swap(i).wait_send()
        sent(q_copy, i)
    sent(log_copy)
    arrive(log_copy)
    share = [shares(i) for i in range(LATE)]
    w_mine(last).wait()
    w_swap(last).wait()
    for i in range(LATE):
        both = merge(i, share[i])
        if early + i < last:
            project(early + i, both)
        else:
            last_att[...] = both
        sent(part_copy, i)


def finish(blocks, acc, att, w, out, rounded, sem):
    width = out.shape[1] // blocks
    copies = []
    for b in range(blocks):
        part = pl.ds(b * width, width)
        total = acc[:, part] + jnp.dot(att[...], w[:, part], preferred_element_type=jnp.float32)
        rounded[:, part] = total.astype(out.dtype)
        copies.append(pltpu.make_async_copy(rounded.at[:, part], out.at[:, part], sem.at[b]))
        copies[-1].start()
    for copy in copies:
        copy.wait()


def on_device(queries, keys, values, tile_lists, out_weight):
    rows, columns = queries.shape
    heads, half, width = columns // HD, rows // 2, out_weight.shape[1]
    early = heads - LATE
    bf16, f32 = jnp.bfloat16, jnp.float32
    anywhere = pl.BlockSpec(memory_space=pl.ANY)
    in_vmem = pl.BlockSpec(memory_space=pltpu.VMEM)
    dma = pltpu.SemaphoreType.DMA
    kept = [
        pltpu.with_memory_space_constraint(x, pltpu.HBM)
        for x in (queries, keys, values, tile_lists.T, out_weight)
    ]
    acc, att, w = pl.pallas_call(
        functools.partial(attend, heads),
        out_shape=(
            pltpu.VMEM((half, width), f32),
            pltpu.VMEM((half, 2 * HD), bf16),
            pltpu.VMEM((2 * HD, width), bf16),
        ),
        in_specs=[pl.BlockSpec(memory_space=pltpu.HBM)] * 5,
        out_specs=(in_vmem, in_vmem, in_vmem),
        scratch_shapes=[
            pltpu.VMEM((rows, columns), bf16),
            pltpu.VMEM((LATE, 2, rows, HD), bf16),
            pltpu.VMEM((2, 3, rows, columns), bf16),
            pltpu.VMEM((heads - 1, 2 * HD, width), bf16),
            pltpu.VMEM((rows, HD), bf16),
            pltpu.VMEM((early, half, HD), bf16),
            pltpu.VMEM((early, half, 2 * HD), bf16),
            pltpu.VMEM((LATE, 2, 2, HD, half), bf16),
            pltpu.VMEM((LATE, 2, 2 * HD, half), bf16),
            pltpu.VMEM((LATE, 2, 2 * HD, half), bf16),
            pltpu.VMEM((LATE, 2, HD, half), f32),
            pltpu.VMEM((LATE, 2 * HD, half), f32),
            pltpu.VMEM((2, 3, LATE, 1, half), f32),
            pltpu.VMEM((3, 2, LATE, 1, half), f32),
            pltpu.VMEM((2, 2, LATE, 1, half), f32),
            pltpu.VMEM((2, RELAYED, HD), bf16),
            pltpu.SMEM(kept[3].shape, jnp.int32),
            dma((4,)),
            dma((early * 4,)),
            dma((early * 4,)),
            dma((LATE * 2,)),
            dma((LATE * 2,)),
            dma((early,)),
            dma((early,)),
            dma((heads,)),
            dma((heads,)),
            dma((heads,)),
            dma((LATE,)),
            dma((LATE,)),
            dma((LATE,)),
            dma((LATE,)),
            dma((LATE * 2,)),
            dma((LATE * 2,)),
            dma((2,)),
            dma((2,)),
            dma,
            dma,
            dma((2,)),
            dma((2,)),
            dma((2,)),
            dma((2,)),
        ],
        compiler_params=pltpu.CompilerParams(
            collective_id=0, has_side_effects=True, vmem_limit_bytes=48 << 20
        ),
        name="attend",
    )(*kept)
    blocks = 4
    return pl.pallas_call(
        functools.partial(finish, blocks),
        out_shape=jax.ShapeDtypeStruct((half, width), bf16),
        in_specs=[in_vmem] * 3,
        out_specs=anywhere,
        scratch_shapes=[pltpu.VMEM((half, width), bf16), dma((blocks,))],
        name="finish",
    )(*(pltpu.with_memory_space_constraint(x, pltpu.VMEM) for x in (acc, att, w)))


def solution(mesh):
    placed = (
        P(("dp", "seq"), "head"),
        P(("dp", "seq"), "head"),
        P(("dp", "seq"), "head"),
        P(),
        P("head", None),
    )
    return jax.shard_map(
        on_device,
        mesh=mesh,
        in_specs=placed,
        out_specs=P(("dp", "seq", "head"), None),
        check_vma=False,
    )
```
